32 devices in a mesh: ctx: 8 (over z, x), head: 4 (over y, core).
Axes of the slice: x: 2, y: 2, z: 4, core: 2. Of those that a mesh axis runs over, the one named last changes fastest.
Arguments:
- queries: bfloat16 [8192, 4096], P('ctx', 'head'), may hold values from -104 to 104
- cache_keys: bfloat16 [3072, 4096], P('ctx', 'head'), may hold values from -4 to 4
- cache_values: bfloat16 [3072, 4096], P('ctx', 'head'), may hold values from -6 to 6
- reflect: bfloat16 [8, 32, 64, 128], P('ctx', 'head'), may hold values from -6 to 6
- betas: bfloat16 [8, 32, 64], P('ctx', 'head'), may hold values from 0.099609375 to 1.8984375
- chain_len: int32 [8], P('ctx'), may hold values from 4 to 8, as said below
- block_start: int32 [8, 4], P('ctx'), may hold values from 0 to 128
- live_len: int32 [8], P('ctx'), may hold values from 1 to 384
- w_out: bfloat16 [4096, 4096], P('head'), may hold values from -0.75 to 0.75
Outputs:
- projected: bfloat16 [8192, 4096], P('ctx', 'head')
The draws below stay inside these ranges and needn't reach their ends.
Inputs may be any that keep to these rules, and one draw needn't show every extreme that they name: `chain_len`: every draw holds a request with 8 shards and one with 4.
All inputs are finite; a program needn't handle non-finite values.
Results may differ from the reference program's by a relative error of at most 0.012.
Values may be sent and summed in bfloat16 or wider, within the bound.
A program may use at most 128 MiB of HBM per device.

```python
import jax
import jax.numpy as jnp
from jax import lax

D = 4096
H = 32
DH = 128
SHARD = 384
QB = 256
NQB = 4
RANK = 64
CHAIN = 8
ROWS = 8192
KEYS = 3072
N_CTX = 8
N_HEAD = 4


def key_table(key):
    samples = jax.random.truncated_normal(jax.random.fold_in(key, 101), -4.0, 4.0, (KEYS, D), jnp.float32)
    return samples


def draw_cache_keys(key, part):
    return key_table(key).astype(jnp.bfloat16)


def draw_queries(key, part):
    samples = 1.5 * jax.random.truncated_normal(jax.random.fold_in(key, 202), -4.0, 4.0, (ROWS, D), jnp.float32)
    return samples.astype(jnp.bfloat16)


def draw_chain_len(key, part):
    levels = jax.random.randint(jax.random.fold_in(key, 404), (N_CTX,), 0, 6)
    lengths = jnp.minimum(4 + levels * levels // 5, CHAIN)
    longest = jax.random.randint(jax.random.fold_in(key, 505), (), 0, N_CTX)
    offset = jax.random.randint(jax.random.fold_in(key, 606), (), 1, N_CTX)
    lengths = lengths.at[longest].set(CHAIN)
    lengths = lengths.at[(longest + offset) % N_CTX].set(4)
    return lengths.astype(jnp.int32)


def plant(values, rng, smallest, high):
    place = [jax.random.randint(jax.random.fold_in(rng, axis), (), 0, length) for axis, length in enumerate(values.shape)]
    main_axis = values.shape.index(max(values.shape))
    neighbour = place[:main_axis] + [(place[main_axis] + 1) % values.shape[main_axis]] + place[main_axis + 1:]
    return values.at[tuple(place)].set(smallest).at[tuple(neighbour)].set(high)


def block_levels(rng, extent, cuts, low, high):
    loudness, own = 1.0, jax.random.fold_in(rng, 6)
    for position, parts in cuts:
        heights = jnp.exp(jax.random.uniform(jax.random.fold_in(own, position), (parts,), jnp.float32, low / len(cuts), high / len(cuts)))
        loudness = loudness * jnp.repeat(heights, extent[position] // parts).reshape([-1 if axis == position else 1 for axis in range(len(extent))])
    return loudness


def normal_values(key, shape, scale, reach, split=(), held_as=jnp.bfloat16):
    drawn = scale * jax.random.normal(key, shape, jnp.float32)
    if split:
        drawn = drawn * block_levels(key, shape, split, -0.22, 0.18)
    return jnp.clip(drawn, -reach, reach).astype(held_as)


def setup_inputs(seed: int = 0) -> dict:
    seeds = jax.random.split(jax.random.key(seed), 10)
    return {
        "queries": draw_queries(jax.random.fold_in(seeds[9], 71), 0),
        "cache_keys": draw_cache_keys(jax.random.fold_in(seeds[9], 71), 0),
        "cache_values": normal_values(seeds[2], (KEYS, D), 1.0, 6.0, ((0, 8), (1, 4))),
        "reflect": normal_values(seeds[3], (N_CTX, H, RANK, DH), 1.0, 6.0, ((0, 8), (1, 4))),
        "betas": jnp.clip(0.099609375 + 1.7988281 * jax.random.uniform(seeds[4], (N_CTX, H, RANK), jnp.float32) ** block_levels(seeds[4], (N_CTX, H, RANK), ((0, 8), (1, 4)), -0.2, 0.2), 0.099609375, 1.8984375).astype(jnp.bfloat16),
        "chain_len": draw_chain_len(jax.random.fold_in(seeds[9], 71), 0),
        "block_start": plant(jax.random.randint(seeds[6], (N_CTX, NQB), 0, SHARD - QB + 1), jax.random.fold_in(seeds[6], 1), 0, SHARD - QB).astype(jnp.int32),
        "live_len": plant(jax.random.randint(seeds[7], (N_CTX,), 1, SHARD + 1), jax.random.fold_in(seeds[7], 1), 1, SHARD).astype(jnp.int32),
        "w_out": normal_values(seeds[8], (D, D), (D // 64) ** -0.5, 0.75, ((0, 4),)),
    }


def rounded(tensor):
    return lax.optimization_barrier(tensor.astype(jnp.bfloat16)).astype(jnp.float32)

def shard_products(reflect, betas):
    unit_rows = reflect.astype(jnp.float32)
    unit_rows = unit_rows / jnp.sqrt(lax.optimization_barrier(jnp.sum(unit_rows * unit_rows, axis=-1, keepdims=True)) + 1e-06)
    rates = betas.astype(jnp.float32)
    initial = jnp.broadcast_to(jnp.eye(DH, dtype=jnp.float32), (N_CTX, H, DH, DH))

    def reflect_once(product, column):
        vector = lax.dynamic_index_in_dim(unit_rows, column, 2, keepdims=False)
        weight = lax.dynamic_index_in_dim(rates, column, 2, keepdims=False)
        applied = jnp.einsum('shij,shj->shi', product, vector, precision=lax.Precision.HIGHEST)
        return (product - weight[:, :, None, None] * applied[:, :, :, None] * vector[:, :, None, :], None)
    product, unused = lax.scan(reflect_once, initial, jnp.arange(RANK))
    return product

def reference(queries, cache_keys, cache_values, reflect, betas, chain_len, block_start, live_len, w_out):
    products = shard_products(reflect, betas)
    key_layout = cache_keys.reshape(N_CTX, SHARD, H, DH)
    value_layout = cache_values.reshape(N_CTX, SHARD, H, DH)
    query_layout = queries.reshape(N_CTX, NQB * QB, H, DH)
    request_rows = NQB * QB
    scale = DH ** (-0.5)
    key_index = jnp.arange(SHARD)
    group_width = D // N_HEAD

    def one_request(request):
        carried = lax.dynamic_index_in_dim(query_layout, request, 0, keepdims=False).astype(jnp.float32)
        positions = (block_start[request][:, None] + jnp.arange(QB)[None, :]).reshape(request_rows)
        length = chain_len[request]
        live_count = live_len[request]
        initial = (carried, jnp.full((H, request_rows), -jnp.inf, jnp.float32), jnp.zeros((H, request_rows), jnp.float32), jnp.zeros((request_rows, H, DH), jnp.float32))

        def visit(carry, distance):
            carried, row_top, row_total, summed = carry
            shard_id = (request - distance) % N_CTX
            shard_keys = lax.dynamic_index_in_dim(key_layout, shard_id, 0, keepdims=False).astype(jnp.float32)
            shard_values = lax.dynamic_index_in_dim(value_layout, shard_id, 0, keepdims=False).astype(jnp.float32)
            active = distance < length
            allowed = jnp.where(distance == 0, key_index[None, :] <= positions[:, None], jnp.where(distance == length - 1, key_index[None, :] >= SHARD - live_count, True))
            allowed = allowed & active
            scores = jnp.einsum('rhd,khd->hrk', rounded(carried), shard_keys) * scale
            scores = jnp.where(allowed[None], scores, -jnp.inf)
            block_top = lax.optimization_barrier(jnp.max(scores, axis=-1))
            safe_top = jnp.where(active, block_top, 0.0)
            weights = rounded(jnp.exp(scores - safe_top[..., None]))
            block_total = lax.optimization_barrier(jnp.sum(weights, axis=-1))
            block_sum = jnp.einsum('hrk,khd->rhd', weights, shard_values)
            new_top = jnp.where(active, jnp.maximum(row_top, block_top), row_top)
            old_factor = jnp.exp(row_top - new_top)
            new_factor = jnp.where(active, jnp.exp(block_top - new_top), 0.0)
            row_total = row_total * old_factor + new_factor * block_total
            summed = summed * old_factor.T[:, :, None] + new_factor.T[:, :, None] * block_sum
            product = lax.dynamic_index_in_dim(products, shard_id, 0, keepdims=False)
            carried = jnp.einsum('rhd,hde->rhe', carried, product, precision=lax.Precision.HIGHEST)
            return ((carried, new_top, row_total, summed), None)
        finished, unused = lax.scan(visit, initial, jnp.arange(CHAIN))
        attended = rounded((finished[3] / finished[2].T[:, :, None]).reshape(request_rows, D))
        outcome = jnp.zeros((request_rows, D), jnp.float32)
        for group in range(N_HEAD):
            columns = attended[:, group * group_width:(group + 1) * group_width]
            weight_rows = w_out[group * group_width:(group + 1) * group_width].astype(jnp.float32)
            outcome = outcome + rounded(jnp.dot(columns, weight_rows, preferred_element_type=jnp.float32))
        return outcome.astype(jnp.bfloat16)
    projected = lax.map(one_request, jnp.arange(N_CTX))
    return projected.reshape(ROWS, D)
```

```python
import functools
import math

import jax
import jax.numpy as jnp
from jax import lax
from jax.experimental import pallas as pl
from jax.experimental.pallas import tpu as pltpu
from jax.sharding import PartitionSpec as P

NT = (((1,), (1,)), ((), ()))
NN = (((1,), (0,)), ((), ()))


def dot32(a, b, dims):
    return lax.dot_general(a, b, dims, preferred_element_type=jnp.float32)


def dot_exact(a, b, dims):
    return lax.dot_general(
        a, b, dims, precision=lax.Precision.HIGHEST, preferred_element_type=jnp.float32
    )


def halves(x):
    high = x.astype(jnp.bfloat16)
    low = (x - high.astype(jnp.float32)).astype(jnp.bfloat16)
    return high, low


def factor_kernel(rank, unit, r_ref, b_ref, w_ref):
    row = lax.broadcasted_iota(jnp.int32, (unit, unit), 0)
    col = lax.broadcasted_iota(jnp.int32, (unit, unit), 1)
    apart = row ^ col
    upper = row < col
    eye = jnp.where(apart == 0, 1.0, 0.0)
    for start in range(0, r_ref.shape[0], unit):
        raw = r_ref[start : start + unit, :].astype(jnp.float32)
        beta = b_ref[start : start + unit, :]
        inverse = 1.0 / jnp.sqrt(jnp.sum(raw * raw, axis=-1, keepdims=True) + 1e-06)
        vectors = raw * inverse
        gram = dot_exact(vectors, vectors, NT)
        coupling = jnp.where(upper & (apart < rank), beta * gram, 0.0)
        solved = eye - jnp.where(apart == 1, coupling, 0.0)
        size = 2
        while size < rank:
            between = jnp.where((apart >= size) & (apart < 2 * size), coupling, 0.0)
            solved = solved - dot_exact(solved, dot_exact(between, solved, NN), NN)
            size *= 2
        w_ref[start : start + unit, :] = inverse * dot_exact(solved, beta * vectors, NN)


def attend_kernel(n, blocks, scal_ref, q_ref, kv_ref, r_ref, w_ref, o_ref, acc_ref, top_ref):
    rows, width = q_ref.shape
    keys = kv_ref.shape[2]
    block = rows // blocks
    rate = math.log2(math.e) / math.sqrt(width)
    me = scal_ref[0]
    length = scal_ref[1]
    live = scal_ref[2]
    ones = jnp.ones((keys, width), jnp.bfloat16)

    def attend(m, turn, mode):
        shard = lax.rem(me - m + n, n)
        shard_keys = kv_ref[shard, 0]
        if turn is not None:
            high, low = halves(turn)
            shard_keys = (dot32(shard_keys, high, NT) + dot32(shard_keys, low, NT)).astype(
                jnp.bfloat16
            )
        extended = jnp.concatenate([kv_ref[shard, 1], ones], axis=1)
        for b in range(blocks):
            here = slice(b * block, (b + 1) * block)
            scores = dot32(q_ref[here, :], shard_keys, NT)
            if mode == 0:
                position = scal_ref[3 + b] + lax.broadcasted_iota(jnp.int32, scores.shape, 0)
                key = lax.broadcasted_iota(jnp.int32, scores.shape, 1)
                scores = jnp.where(key <= position, scores, -jnp.inf)
            if mode == 2:
                key = lax.broadcasted_iota(jnp.int32, scores.shape, 1)
                scores = jnp.where(key >= keys - live, scores, -jnp.inf)
            top = jnp.max(scores, axis=-1, keepdims=True)
            if mode != 0:
                before = top_ref[here, :]
                top = jnp.maximum(top, before)
            weights = jnp.exp2((scores - top) * rate).astype(jnp.bfloat16)
            part = dot32(weights, extended, NN)
            if mode != 0:
                part = part + acc_ref[here, :] * jnp.exp2((before - top) * rate)
            if mode == 2:
                o_ref[here, :] = (part[:, :width] / part[:, width:]).astype(o_ref.dtype)
            else:
                acc_ref[here, :] = part
                top_ref[here, :] = top

    def advance(m, turn):
        shard = lax.rem(me - m + 1 + n, n)
        vectors = r_ref[shard, 0]
        high, low = halves(turn)
        ahigh, alow = halves(dot32(high, vectors, NT) + dot32(low, vectors, NT))
        whigh, wlow = halves(w_ref[shard, 0])
        return turn - (
            dot32(ahigh, whigh, NN) + (dot32(alow, whigh, NN) + dot32(ahigh, wlow, NN))
        )

    row = lax.broadcasted_iota(jnp.int32, (width, width), 0)
    col = lax.broadcasted_iota(jnp.int32, (width, width), 1)
    eye = jnp.where(row == col, 1.0, 0.0).astype(jnp.float32)
    attend(0, None, 0)

    def step(m, turn):
        turn = advance(m, turn)
        attend(m, turn, 1)
        return turn

    turn = lax.fori_loop(1, length - 1, step, eye)
    attend(length - 1, advance(length - 1, turn), 2)


def shards(queries, cache_keys, cache_values, reflect, betas, chain_len, block_start, live_len, w_out):
    rows = queries.shape[0]
    heads, rank, width = reflect.shape[1:]
    keys = cache_keys.shape[0]
    blocks = block_start.shape[1]
    n = lax.axis_size("ctx")
    groups = lax.axis_size("head")
    me = lax.axis_index("ctx")
    group = lax.axis_index("head")
    chunks = 4
    per = heads // chunks
    columns = w_out.shape[1] // groups

    per_unit = max(1, min(heads, 256 // rank))
    factors = pl.pallas_call(
        functools.partial(factor_kernel, rank, per_unit * rank),
        out_shape=jax.ShapeDtypeStruct((heads * rank, width), jnp.float32),
        compiler_params=pltpu.CompilerParams(vmem_limit_bytes=40 * 2**20),
        name="factors",
    )(
        reflect[0].reshape(heads * rank, width),
        betas[0].astype(jnp.float32).reshape(heads * rank, 1),
    )
    all_reflect = lax.all_gather(reflect[0], "ctx")
    all_factors = lax.all_gather(factors.reshape(heads, rank, width), "ctx")
    gathered = []
    for chunk in range(chunks):
        cut = slice(chunk * per * width, (chunk + 1) * per * width)
        gathered.append(lax.all_gather(jnp.stack([cache_keys[:, cut], cache_values[:, cut]]), "ctx"))

    pieces = [lax.dynamic_slice_in_dim(w_out, group * columns, columns, 1)]
    for shift in range(1, groups):
        piece = lax.dynamic_slice_in_dim(
            w_out, lax.rem(group + shift, groups) * columns, columns, 1
        )
        pieces.append(
            lax.ppermute(piece, "head", [(i, (i + shift) % groups) for i in range(groups)])
        )
    stack = jnp.stack(pieces)

    scalars = jnp.concatenate(
        [me.astype(jnp.int32)[None], chain_len, live_len, block_start[0]]
    )
    outcome = None
    for chunk in range(chunks):
        base = chunk * per
        attended = pl.pallas_call(
            functools.partial(attend_kernel, n, blocks),
            out_shape=jax.ShapeDtypeStruct((rows, per * width), jnp.bfloat16),
            grid_spec=pltpu.PrefetchScalarGridSpec(
                num_scalar_prefetch=1,
                grid=(per,),
                in_specs=[
                    pl.BlockSpec((rows, width), lambda h, s, base=base: (0, base + h)),
                    pl.BlockSpec((n, 2, keys, width), lambda h, s: (0, 0, 0, h)),
                    pl.BlockSpec((n, 1, rank, width), lambda h, s, base=base: (0, base + h, 0, 0)),
                    pl.BlockSpec((n, 1, rank, width), lambda h, s, base=base: (0, base + h, 0, 0)),
                ],
                out_specs=pl.BlockSpec((rows, width), lambda h, s: (0, h)),
                scratch_shapes=[
                    pltpu.VMEM((rows, 2 * width), jnp.float32),
                    pltpu.VMEM((rows, 1), jnp.float32),
                ],
            ),
            compiler_params=pltpu.CompilerParams(vmem_limit_bytes=40 * 2**20),
            cost_estimate=pl.CostEstimate(
                flops=per * 16 * rows * keys * width * 2,
                bytes_accessed=per * (16 * keys * width * 2 + 4 * rows * width),
                transcendentals=per * 8 * rows * keys,
            ),
            name="attend",
        )(scalars, queries, gathered[chunk], all_reflect, all_factors)
        shared = lax.all_gather(attended, "head", axis=1, tiled=True)
        share = jnp.concatenate(
            [
                lax.dynamic_slice(
                    stack,
                    (lax.rem(group - g + groups, groups), base * width, 0),
                    (1, per * width, columns),
                )[0]
                for g in range(groups)
            ]
        )
        term = jnp.dot(shared, share, preferred_element_type=jnp.float32)
        outcome = term if outcome is None else outcome + term
    return outcome.astype(jnp.bfloat16)


def solution(mesh):
    return jax.shard_map(
        shards,
        mesh=mesh,
        in_specs=(
            P("ctx", "head"),
            P("ctx", "head"),
            P("ctx", "head"),
            P("ctx", "head", None, None),
            P("ctx", "head", None),
            P("ctx"),
            P("ctx", None),
            P("ctx"),
            P("head", None),
        ),
        out_specs=P("ctx", "head"),
        check_vma=False,
    )
```
